128 devices in a mesh: ctx: 64 (over z, y, x), head: 2 (over core).
Axes of the slice: x: 4, y: 4, z: 4, core: 2. Of those that a mesh axis runs over, the one named last changes fastest.
Arguments:
- queries: bfloat16 [16384, 4096], P('ctx', 'head'), may hold values from -6 to 6
- keys: bfloat16 [16384, 4096], P('ctx', 'head'), may hold values from -6 to 6
- values: bfloat16 [16384, 4096], P('ctx', 'head'), may hold values from -6 to 6
- log_decay: float32 [32, 16384], P('head', 'ctx'), may hold values from -0.8 to 0, as said below
- norm_gain: float32 [4096], P('head'), may hold values from 0.1 to 1.9
- d_out: bfloat16 [16384, 4096], P('ctx', 'head'), may hold values from -6 to 6
Outputs:
- output: bfloat16 [16384, 4096], P('ctx', 'head')
- grad_queries: bfloat16 [16384, 4096], P('ctx', 'head')
- grad_keys: bfloat16 [16384, 4096], P('ctx', 'head')
- grad_values: bfloat16 [16384, 4096], P('ctx', 'head')
The draws below stay inside these ranges and needn't reach their ends.
Inputs may be any that keep to these rules, and one draw needn't show every extreme that they name: log_decay is negative everywhere.
All inputs are finite; a program needn't handle non-finite values.
Results may differ from the reference program's by a relative error of at most 0.014.
Values may be sent and summed in bfloat16 or wider, within the bound.
A program may use at most 192 MiB of HBM per device.

```python
import math
import jax
import jax.numpy as jnp
from jax import lax

DH = 128
TOK_DEV = 256
HEADS = 32
LENGTH = 16384


def draw_log_decay(key, part):
    key = jax.random.fold_in(key, 11)
    streams = jax.random.split(key, 8)
    fast_share = 0.5
    picks = jax.random.uniform(streams[0], (HEADS, 1))
    fast_rate = jnp.exp(jax.random.uniform(streams[1], (HEADS, 1), minval=math.log(1.0 / 50.0), maxval=math.log(1.0 / 30.0)))
    slow_rate = math.log(10.0) / (8.0 * LENGTH) * jnp.exp(jax.random.uniform(streams[2], (HEADS, 1), minval=-0.5, maxval=0.5))
    baseline_decay_rate = jnp.where(picks < fast_share, fast_rate, slow_rate)
    block_each = jnp.exp(jax.random.uniform(streams[3], (HEADS, LENGTH // TOK_DEV), minval=math.log(0.5), maxval=math.log(1.5)))
    block_each = jnp.repeat(block_each, TOK_DEV, axis=1)
    jitter_level = jax.random.uniform(streams[4], (HEADS, LENGTH), minval=0.5, maxval=1.5)
    leading_location = jax.random.randint(streams[5], (), 0, LENGTH)
    trailing_location = (leading_location + 1 + jax.random.randint(streams[7], (), 0, LENGTH - 1)) % LENGTH
    layer_depth = jax.random.uniform(streams[6], (HEADS, 2), minval=math.log(0.5), maxval=math.log(0.8))
    token_place = jnp.arange(LENGTH)[None, :]
    spike_events = jnp.where(token_place == leading_location, layer_depth[:, 0:1], 0.0) + jnp.where(token_place == trailing_location, layer_depth[:, 1:2], 0.0)
    return (spike_events - baseline_decay_rate * block_each * jitter_level).astype(jnp.float32)


def levels(key, extent, shards, smallest, top_value):
    def one(axis_at, parts):
        heights = jax.random.uniform(jax.random.fold_in(jax.random.fold_in(key, 6), axis_at), (parts,), jnp.float32, smallest / len(shards), top_value / len(shards))
        return jnp.repeat(jnp.exp(heights), extent[axis_at] // parts).reshape((-1,) + (1,) * (len(extent) - axis_at - 1))

    factor_of = one(*shards[0])
    for cut in shards[1:]:
        factor_of = factor_of * one(*cut)
    return factor_of


def centred(key, dims, deviation, bound, cuts=(), held_as=jnp.bfloat16):
    result = deviation * jax.random.normal(key, dims, jnp.float32)
    if cuts:
        result = result * levels(key, dims, cuts, -0.22, 0.18)
    return jnp.clip(result, -bound, bound).astype(held_as)


def setup_inputs(seed: int = 0) -> dict:
    key_of = jax.random.split(jax.random.key(seed), 7)
    return {
        "queries": centred(key_of[0], (LENGTH, HEADS * DH), 1.0, 6.0, ((0, 64), (1, 2))),
        "keys": centred(key_of[1], (LENGTH, HEADS * DH), 1.0, 6.0, ((0, 64), (1, 2))),
        "values": centred(key_of[2], (LENGTH, HEADS * DH), 1.0, 6.0, ((0, 64), (1, 2))),
        "log_decay": draw_log_decay(jax.random.fold_in(key_of[6], 71), 0),
        "norm_gain": jnp.clip(1.0 + 0.18 * jax.random.normal(key_of[4], (HEADS * DH,), jnp.float32), 0.1, 1.9),
        "d_out": centred(key_of[5], (LENGTH, HEADS * DH), 1.0, 6.0, ((0, 64), (1, 2))),
    }


EPSILON = 1e-06

def decay_matrix(cumulative):
    length_here = cumulative.shape[-1]
    rows_index = jnp.arange(length_here)[:, None]
    cols_index = jnp.arange(length_here)[None, :]
    spread = cumulative[:, :, None] - cumulative[:, None, :]
    return jnp.exp(jnp.where(rows_index >= cols_index, spread, -1e+30))

def lowered(state):
    return lax.optimization_barrier(state.astype(jnp.bfloat16)).astype(jnp.float32)

def reference(queries, keys, values, log_decay, norm_gain, d_out):
    seq_len, full_width = queries.shape
    head_count = full_width // DH
    blocks = seq_len // TOK_DEV

    def split_heads(array):
        return array.reshape(blocks, TOK_DEV, head_count, DH).transpose(0, 2, 1, 3)

    def join_heads(array):
        return array.transpose(0, 2, 1, 3).reshape(seq_len, full_width)
    queries_b = split_heads(queries)
    keys_b = split_heads(keys)
    values_b = split_heads(values)
    cumulative = jnp.cumsum(log_decay.reshape(head_count, blocks, TOK_DEV).transpose(1, 0, 2), axis=2)

    def forward_step(carried, pieces):
        query_blk, key_blk, value_blk, cum_blk = pieces
        scores = jnp.einsum('htd,hsd->hts', query_blk.astype(jnp.float32), key_blk.astype(jnp.float32))
        weights = (scores * decay_matrix(cum_blk)).astype(jnp.bfloat16)
        attn = jnp.exp(cum_blk)[:, :, None] * jnp.einsum('htd,hde->hte', query_blk.astype(jnp.float32), lowered(carried))
        attn = attn + jnp.einsum('hts,hse->hte', weights.astype(jnp.float32), value_blk.astype(jnp.float32))
        trail = jnp.exp(cum_blk[:, -1:] - cum_blk)[:, :, None]
        decayed_keys = (key_blk.astype(jnp.float32) * trail).astype(jnp.bfloat16)
        own_state = jnp.einsum('htd,hte->hde', decayed_keys.astype(jnp.float32), value_blk.astype(jnp.float32))
        following = jnp.exp(cum_blk[:, -1])[:, None, None] * carried + own_state
        return (following, (attn, carried))
    start = jnp.zeros((head_count, DH, DH), jnp.float32)
    _, (attn, entering) = lax.scan(forward_step, start, (queries_b, keys_b, values_b, cumulative))
    gain = norm_gain.astype(jnp.float32).reshape(head_count, DH)[None, :, None, :]
    scale = lax.rsqrt(lax.optimization_barrier(jnp.mean(attn * attn, axis=(1, 3), keepdims=True)) + EPSILON)
    normed = attn * scale
    output = (normed * gain).astype(jnp.bfloat16)
    grad_gain = gain * split_heads(d_out).astype(jnp.float32)
    inner_mean = lax.optimization_barrier(jnp.mean(normed * grad_gain, axis=(1, 3), keepdims=True))
    d_attn = (scale * (grad_gain - normed * inner_mean)).astype(jnp.bfloat16)

    def backward_step(carried, pieces):
        query_blk, key_blk, value_blk, cum_blk, grad_blk, entering_blk = pieces
        decay = decay_matrix(cum_blk)
        queries_f = query_blk.astype(jnp.float32)
        keys_f = key_blk.astype(jnp.float32)
        values_f = value_blk.astype(jnp.float32)
        grad_f = grad_blk.astype(jnp.float32)
        weights = (jnp.einsum('htd,hsd->hts', queries_f, keys_f) * decay).astype(jnp.bfloat16)
        grad_weights = (jnp.einsum('htd,hsd->hts', grad_f, values_f) * decay).astype(jnp.bfloat16)
        lead = jnp.exp(cum_blk)[:, :, None]
        trail = jnp.exp(cum_blk[:, -1:] - cum_blk)[:, :, None]
        entering_low = lowered(entering_blk)
        leaving_low = lowered(carried)
        grad_query = lead * jnp.einsum('hte,hde->htd', grad_f, entering_low)
        grad_query = grad_query + jnp.einsum('hts,hsd->htd', grad_weights.astype(jnp.float32), keys_f)
        grad_key = trail * jnp.einsum('hte,hde->htd', values_f, leaving_low)
        grad_key = grad_key + jnp.einsum('hts,htd->hsd', grad_weights.astype(jnp.float32), queries_f)
        grad_value = trail * jnp.einsum('htd,hde->hte', keys_f, leaving_low)
        grad_value = grad_value + jnp.einsum('hts,hte->hse', weights.astype(jnp.float32), grad_f)
        decayed_queries = (queries_f * lead).astype(jnp.bfloat16)
        own_grad = jnp.einsum('htd,hte->hde', decayed_queries.astype(jnp.float32), grad_f)
        following = own_grad + jnp.exp(cum_blk[:, -1])[:, None, None] * carried
        return (following, (grad_query.astype(jnp.bfloat16), grad_key.astype(jnp.bfloat16), grad_value.astype(jnp.bfloat16)))
    _, (grad_q, grad_k, grad_v) = lax.scan(backward_step, start, (queries_b, keys_b, values_b, cumulative, d_attn, entering), reverse=True)
    return (join_heads(output), join_heads(grad_q), join_heads(grad_k), join_heads(grad_v))
```

```python
import functools

import jax
import jax.numpy as jnp
from jax import lax
from jax.experimental import pallas as pl
from jax.experimental.pallas import tpu as pltpu
from jax.sharding import PartitionSpec as P

DH = 128
EPSILON = 1e-06
MESH = pl.DeviceIdType.MESH
F32 = jnp.float32
BF16 = jnp.bfloat16


def dot(a, b, dims):
    return lax.dot_general(a, b, (dims, ((), ())), preferred_element_type=F32)


NN = ((1,), (0,))
NT = ((1,), (1,))
TN = ((0,), (0,))


def kernel(
    n, heads, pos,
    q_hbm, k_hbm, v_hbm, ld_hbm, gain_hbm, g_hbm,
    out_hbm, gq_hbm, gk_hbm, gv_hbm,
    q, k, v, g, ld, gain,
    cum, cumb, leadb, trailb, decay, weights, dk, ql,
    attn, d_attn, out, gq, gk, gv,
    s_send, s_recv, e_send, e_recv, t_send, t_recv, l_send, l_recv,
    totals, block_decay, sums, sums_in,
    in_sem, out_sem, sems, sum_sem,
):
    c = lax.axis_index("ctx")
    core = lax.axis_index("head")
    rows = DH * heads // n
    per_head = n // heads
    side = 8
    c_hi, c_lo = c // side, c % side
    width = heads * DH

    loads = [
        pltpu.make_async_copy(src, dst, in_sem.at[i])
        for i, (src, dst) in enumerate(
            ((ld_hbm, ld), (k_hbm, k), (v_hbm, v), (q_hbm, q), (gain_hbm, gain), (g_hbm, g))
        )
    ]
    for load in loads:
        load.start()

    barrier = pltpu.get_barrier_semaphore()

    def greet(i, _):
        pl.semaphore_signal(
            barrier, inc=1, device_id=((c + i) % n, core), device_id_type=MESH
        )
        return 0

    lax.fori_loop(1, n, greet, 0)
    pl.semaphore_signal(barrier, inc=1, device_id=(c, 1 - core), device_id_type=MESH)

    def lanes(h):
        return pl.ds(pl.multiple_of(h * DH, DH), DH)

    def share_copy(src, dst, which, dest):
        return pltpu.make_async_remote_copy(
            src_ref=src.at[dest],
            dst_ref=dst.at[c],
            send_sem=sems.at[2 * which],
            recv_sem=sems.at[2 * which + 1],
            device_id=(dest, core),
            device_id_type=MESH,
        )

    def send_shares(src, dst, which):
        def one(i, _):
            share_copy(src, dst, which, (c + i) % n).start()
            return 0

        lax.fori_loop(1, n, one, 0)
        dst[c] = src[c]

    def all_shares(src, dst, which):
        return pltpu.make_async_remote_copy(
            src_ref=src.at[pl.ds(0, n - 1)],
            dst_ref=dst.at[pl.ds(0, n - 1)],
            send_sem=sems.at[2 * which],
            recv_sem=sems.at[2 * which + 1],
            device_id=((c + 1) % n, core),
            device_id_type=MESH,
        )

    loads[0].wait()
    t_i = lax.broadcasted_iota(jnp.int32, (pos, pos), 0)
    s_i = lax.broadcasted_iota(jnp.int32, (pos, pos), 1)
    lower = jnp.where(t_i >= s_i, 1.0, 0.0).astype(BF16)
    ld_all = jnp.concatenate([ld[...], jnp.zeros((DH - heads, pos), F32)], axis=0)
    hi = ld_all.astype(BF16)
    rest = ld_all - hi.astype(F32)
    mid = rest.astype(BF16)
    low = (rest - mid.astype(F32)).astype(BF16)
    cum_t = dot(lower, hi, NT) + dot(lower, mid, NT) + dot(lower, low, NT)
    cum_h = dot(hi, lower, NT) + dot(mid, lower, NT) + dot(low, lower, NT)
    cum[...] = cum_h[:heads]
    last = cum_t[pos - 1 : pos, :]
    trail_t = jnp.exp(last - cum_t)
    for h in range(heads):
        trailb[h] = jnp.broadcast_to(trail_t[:, h : h + 1], (pos, DH))
    totals[c_hi, c_lo] = last

    loads[1].wait()
    loads[2].wait()

    def own_state(h, _):
        keys = (k[:, lanes(h)].astype(F32) * trailb[h]).astype(BF16)
        dk[:, lanes(h)] = keys
        state = dot(keys, v[:, lanes(h)], TN).astype(BF16)
        s_send[pl.ds(h * per_head, per_head)] = state.reshape(per_head, rows, DH)
        return 0

    lax.fori_loop(0, heads, own_state, 0, unroll=2)

    pl.semaphore_wait(barrier, n)

    def totals_row(i):
        return pltpu.make_async_remote_copy(
            src_ref=totals.at[c_hi, c_lo],
            dst_ref=totals.at[c_hi, c_lo],
            send_sem=sum_sem.at[2],
            recv_sem=sum_sem.at[3],
            device_id=(c_hi * side + (c_lo + i) % side, core),
            device_id_type=MESH,
        )

    def totals_rows(i):
        return pltpu.make_async_remote_copy(
            src_ref=totals.at[c_hi],
            dst_ref=totals.at[c_hi],
            send_sem=sum_sem.at[4],
            recv_sem=sum_sem.at[5],
            device_id=(((c_hi + i) % side) * side + c_lo, core),
            device_id_type=MESH,
        )

    for i in range(1, side):
        totals_row(i).start()
    send_shares(s_send, s_recv, 0)

    lead_t = jnp.exp(cum_t)
    for h in range(heads):
        cumb[h] = jnp.broadcast_to(cum_t[:, h : h + 1], (pos, DH))
        leadb[h] = jnp.broadcast_to(lead_t[:, h : h + 1], (pos, DH))

    some = pltpu.make_async_remote_copy(
        src_ref=totals.at[0, pl.ds(0, side - 1)],
        dst_ref=totals.at[0, pl.ds(0, side - 1)],
        send_sem=sum_sem.at[2],
        recv_sem=sum_sem.at[3],
        device_id=((c + 1) % n, core),
        device_id_type=MESH,
    )
    some.wait()
    for i in range(1, side):
        totals_rows(i).start()

    loads[3].wait()

    def inside(h, _):
        scores = dot(q[:, lanes(h)], k[:, lanes(h)], NT)
        row = cum[pl.ds(h, 1), :]
        col = cumb[h]
        spread = jnp.concatenate([col, col], axis=1) - row
        d = jnp.exp(jnp.where(t_i >= s_i, spread, -1e30))
        decay[h] = d
        w = (scores * d).astype(BF16)
        weights[h] = w
        attn[:, lanes(h)] = dot(w, v[:, lanes(h)], NN)
        ql[:, lanes(h)] = (q[:, lanes(h)].astype(F32) * leadb[h]).astype(BF16)
        return 0

    lax.fori_loop(0, heads, inside, 0, unroll=2)

    some = pltpu.make_async_remote_copy(
        src_ref=totals.at[pl.ds(0, side - 1)],
        dst_ref=totals.at[pl.ds(0, side - 1)],
        send_sem=sum_sem.at[4],
        recv_sem=sum_sem.at[5],
        device_id=((c + 1) % n, core),
        device_id_type=MESH,
    )
    some.wait()
    every = totals[...].reshape(n, DH)
    lane_i = lax.broadcasted_iota(jnp.int32, (n, DH), 1)
    mine = jnp.sum(jnp.where(lane_i == c // per_head, every, 0.0), axis=1, keepdims=True)
    block_decay[...] = jnp.broadcast_to(jnp.exp(mine), (n, DH))

    def scan(src, dst, reverse):
        def one(i, state):
            j = n - 1 - i if reverse else i
            dst[j] = state.astype(BF16)
            return state * block_decay[pl.ds(j, 1), :] + src[j].astype(F32)

        lax.fori_loop(0, n, one, jnp.zeros((rows, DH), F32), unroll=8)

    all_shares(s_send, s_recv, 0).wait()
    scan(s_recv, e_send, False)
    send_shares(e_send, e_recv, 1)
    loads[4].wait()
    loads[5].wait()
    all_shares(e_send, e_recv, 1).wait()

    def attend(h, carry):
        squares, inner = carry
        entering = e_recv[pl.ds(h * per_head, per_head)].reshape(DH, DH)
        a = attn[:, lanes(h)] + leadb[h] * dot(q[:, lanes(h)], entering, NN)
        attn[:, lanes(h)] = a
        gg = gain[:, lanes(h)] * g[:, lanes(h)].astype(F32)
        return squares + a * a, inner + a * gg

    zero = jnp.zeros((pos, DH), F32)
    squares, inner = lax.fori_loop(0, heads, attend, (zero, zero), unroll=2)
    squares = jnp.sum(squares, axis=1, keepdims=True)
    inner = jnp.sum(inner, axis=1, keepdims=True)
    half_i = lax.broadcasted_iota(jnp.int32, (pos, DH), 1)
    sums[...] = jnp.where(half_i < DH // 2, squares, inner)
    swap = pltpu.make_async_remote_copy(
        src_ref=sums,
        dst_ref=sums_in,
        send_sem=sum_sem.at[0],
        recv_sem=sum_sem.at[1],
        device_id=(c, 1 - core),
        device_id_type=MESH,
    )
    swap.start()
    swap.wait()
    both = sums[...] + sums_in[...]
    full = 2 * width
    scale = lax.rsqrt(both[:, 0:1] / full + EPSILON)
    pull = scale * scale * (both[:, DH - 1 : DH] / full)
    scale = jnp.broadcast_to(scale, (pos, DH))
    pull = jnp.broadcast_to(pull, (pos, DH))
    sums[...] = scale

    def own_grad(h, _):
        a = attn[:, lanes(h)]
        gg = gain[:, lanes(h)] * g[:, lanes(h)].astype(F32)
        d = (scale * (gg - a * pull)).astype(BF16)
        d_attn[:, lanes(h)] = d
        state = dot(ql[:, lanes(h)], d, TN).astype(BF16)
        t_send[pl.ds(h * per_head, per_head)] = state.reshape(per_head, rows, DH)
        return 0

    lax.fori_loop(0, heads, own_grad, 0, unroll=2)
    send_shares(t_send, t_recv, 2)

    def gradients(h, _):
        d = d_attn[:, lanes(h)]
        out[:, lanes(h)] = (attn[:, lanes(h)] * sums[...] * gain[:, lanes(h)]).astype(BF16)
        w = weights[h]
        gw = (dot(d, v[:, lanes(h)], NT) * decay[h]).astype(BF16)
        entering = e_recv[pl.ds(h * per_head, per_head)].reshape(DH, DH)
        gq[:, lanes(h)] = (
            leadb[h] * dot(d, entering, NT) + dot(gw, k[:, lanes(h)], NN)
        ).astype(BF16)
        attn[:, lanes(h)] = dot(gw, q[:, lanes(h)], TN)
        decay[h, :, 0:DH] = dot(w, d, TN)
        return 0

    lax.fori_loop(0, heads // 2, gradients, 0)
    all_shares(t_send, t_recv, 2).wait()
    scan(t_recv, l_send, True)
    send_shares(l_send, l_recv, 3)
    lax.fori_loop(heads // 2, heads, gradients, 0)
    stores = [
        pltpu.make_async_copy(src, dst, out_sem.at[i])
        for i, (src, dst) in enumerate(
            ((out, out_hbm), (gq, gq_hbm), (gk, gk_hbm), (gv, gv_hbm))
        )
    ]
    stores[0].start()
    stores[1].start()
    all_shares(l_send, l_recv, 3).wait()

    def finish(h, _):
        leaving = l_recv[pl.ds(h * per_head, per_head)].reshape(DH, DH)
        gk[:, lanes(h)] = (
            attn[:, lanes(h)] + trailb[h] * dot(v[:, lanes(h)], leaving, NT)
        ).astype(BF16)
        gv[:, lanes(h)] = (
            decay[h, :, 0:DH] + trailb[h] * dot(k[:, lanes(h)], leaving, NN)
        ).astype(BF16)
        return 0

    lax.fori_loop(0, heads, finish, 0, unroll=2)
    stores[2].start()
    stores[3].start()
    for store in stores:
        store.wait()


def solution(mesh):
    n = mesh.shape["ctx"]

    def local(queries, keys, values, log_decay, norm_gain, d_out):
        pos, width = queries.shape
        heads = width // DH
        rows = DH * heads // n
        wide = jax.ShapeDtypeStruct((pos, width), BF16)
        anywhere = pl.BlockSpec(memory_space=pl.ANY)
        shares = pltpu.VMEM((n, rows, DH), BF16)
        columns = pltpu.VMEM((heads, pos, DH), F32)
        flat = pltpu.VMEM((pos, width), BF16)
        return pl.pallas_call(
            functools.partial(kernel, n, heads, pos),
            out_shape=[wide] * 4,
            in_specs=[anywhere] * 6,
            out_specs=[anywhere] * 4,
            scratch_shapes=[
                flat, flat, flat, flat,
                pltpu.VMEM((heads, pos), F32),
                pltpu.VMEM((1, width), F32),
                pltpu.VMEM((heads, pos), F32),
                columns, columns, columns,
                pltpu.VMEM((heads, pos, pos), F32),
                pltpu.VMEM((heads, pos, pos), BF16),
                flat, flat,
                pltpu.VMEM((pos, width), F32),
                flat, flat, flat, flat, flat,
                shares, shares, shares, shares, shares, shares, shares, shares,
                pltpu.VMEM((8, n // 8, 1, DH), F32),
                pltpu.VMEM((n, DH), F32),
                pltpu.VMEM((pos, DH), F32),
                pltpu.VMEM((pos, DH), F32),
                pltpu.SemaphoreType.DMA((6,)),
                pltpu.SemaphoreType.DMA((4,)),
                pltpu.SemaphoreType.DMA((8,)),
                pltpu.SemaphoreType.DMA((6,)),
            ],
            compiler_params=pltpu.CompilerParams(
                collective_id=0, has_side_effects=True, vmem_limit_bytes=50 * 2**20
            ),
            cost_estimate=pl.CostEstimate(
                flops=36 * pos * DH * DH * heads, bytes_accessed=16 * pos * width, transcendentals=0
            ),
            name="attention",
        )(queries, keys, values, log_decay, norm_gain.reshape(1, width), d_out)

    wide = P("ctx", "head")
    return jax.shard_map(
        local,
        mesh=mesh,
        in_specs=(wide, wide, wide, P("head", "ctx"), P("head"), wide),
        out_specs=(wide, wide, wide, wide),
        check_vma=False,
    )
```

```python
import functools
import itertools

import jax
import jax.numpy as jnp
from jax import lax
from jax.experimental import pallas as pl
from jax.experimental.pallas import tpu as pltpu
from jax.sharding import PartitionSpec as P

DH = 128
EPSILON = 1e-06
SIDE = 4
SPLIT = (2, 2, 2)
HOPS = (0, 1, 2, 1)
MESH = pl.DeviceIdType.MESH
F32 = jnp.float32
BF16 = jnp.bfloat16
NN = ((1,), (0,))
NT = ((1,), (1,))
TN = ((0,), (0,))


def dot(a, b, dims):
    return lax.dot_general(a, b, (dims, ((), ())), preferred_element_type=F32)


def routes(place, group, split):
    per_axis = []
    for at, chosen, part in zip(place, group, split):
        steps = []
        for turn in range(SIDE // part):
            shift = (chosen - at) % part + part * turn
            hops = sum(HOPS[part * turn + i] for i in range(part)) / part
            steps.append(((at + shift) % SIDE, hops, turn == 0))
        per_axis.append(steps)
    found = []
    for steps in itertools.product(*per_axis):
        ctx, member = 0, 0
        for (at, _, _), part in zip(steps, split):
            ctx = ctx * SIDE + at
            member = member * (SIDE // part) + at // part
        found.append((sum(s[1] for s in steps), ctx, member, all(s[2] for s in steps)))
    found.sort(key=lambda r: -r[0])
    return [r[1:] for r in found]


def kernel(
    n, heads, pos,
    q_hbm, k_hbm, v_hbm, ld_hbm, gain_hbm, g_hbm,
    out, gq, gk, gv,
    q, k, v, g, ld, gain,
    cum, cumb, leadb, trailb, decay, weights, dk, dv, ql, qt,
    attn, gg, d_attn,
    s_send, s_recv, e_send, e_recv, t_send, t_recv, l_send, l_recv,
    totals, block_decay, sums, sums_in,
    in_sem, share_sem, group_sem, sum_sem,
):
    c = lax.axis_index("ctx")
    core = lax.axis_index("head")
    place = (c // (SIDE * SIDE), (c // SIDE) % SIDE, c % SIDE)
    rows = DH * heads // n
    per_head = n // heads
    groups = list(itertools.product(*(range(part) for part in SPLIT)))
    members = n // len(groups)
    group_heads = heads // len(groups)
    my_group, my_member = 0, 0
    for at, part in zip(place, SPLIT):
        my_group = my_group * part + at % part
        my_member = my_member * (SIDE // part) + at // part
    mine = my_group * members + my_member
    width = heads * DH

    loads = [
        pltpu.make_async_copy(src, dst, in_sem.at[i])
        for i, (src, dst) in enumerate(
            ((ld_hbm, ld), (k_hbm, k), (v_hbm, v), (q_hbm, q), (gain_hbm, gain), (g_hbm, g))
        )
    ]
    for load in loads:
        load.start()

    barrier = pltpu.get_barrier_semaphore()

    def greet(i, _):
        pl.semaphore_signal(
            barrier, inc=1, device_id=((c + i) % n, core), device_id_type=MESH
        )
        return 0

    lax.fori_loop(1, n, greet, 0)
    pl.semaphore_signal(barrier, inc=1, device_id=(c, 1 - core), device_id_type=MESH)

    def lanes(h):
        return pl.ds(h * DH, DH) if isinstance(h, int) else pl.ds(pl.multiple_of(h * DH, DH), DH)

    def shares(h):
        return pl.ds(h * per_head, per_head)

    def send(src, dst, sent, landed, dest, maybe_me):
        def away():
            pltpu.make_async_remote_copy(
                src_ref=src, dst_ref=dst, send_sem=sent, recv_sem=landed,
                device_id=(dest, core), device_id_type=MESH,
            ).start()

        if maybe_me:
            pl.when(dest != c)(away)

            @pl.when(dest == c)
            def _():
                pltpu.make_async_copy(src, dst, landed).start()
        else:
            away()

    def to_owners(src, dst, which, group):
        for dest, member, maybe_me in routes(place, groups[group], SPLIT):
            send(
                src.at[group * members + member], dst.at[c],
                share_sem.at[2 * which], share_sem.at[2 * which + 1], dest, maybe_me,
            )

    def from_owner(src, dst, which):
        for dest, _, maybe_me in routes(place, (0, 0, 0), (1, 1, 1)):
            send(
                src.at[dest], dst.at[mine],
                share_sem.at[4 + which], group_sem.at[which, my_group], dest, maybe_me,
            )

    def any_copy(ref, sent, landed):
        return pltpu.make_async_remote_copy(
            src_ref=ref, dst_ref=ref, send_sem=sent, recv_sem=landed,
            device_id=((c + 1) % n, core), device_id_type=MESH,
        )

    def owners_wait(dst, which):
        any_copy(dst, share_sem.at[2 * which], share_sem.at[2 * which + 1]).wait_recv()

    def group_wait(dst, which, group):
        any_copy(
            dst.at[pl.ds(group * members, members)],
            share_sem.at[4 + which], group_sem.at[which, group],
        ).wait_recv()

    def each(first, last, body, unroll):
        def step(h, _):
            body(h)
            return 0

        lax.fori_loop(first, last, step, 0, unroll=unroll)

    loads[0].wait()
    t_i = lax.broadcasted_iota(jnp.int32, (pos, pos), 0)
    s_i = lax.broadcasted_iota(jnp.int32, (pos, pos), 1)
    lower = jnp.where(t_i >= s_i, 1.0, 0.0).astype(BF16)
    ld_all = jnp.concatenate([ld[...], jnp.zeros((DH - heads, pos), F32)], axis=0)
    hi = ld_all.astype(BF16)
    rest = ld_all - hi.astype(F32)
    mid = rest.astype(BF16)
    low = (rest - mid.astype(F32)).astype(BF16)
    cum_t = dot(lower, hi, NT) + dot(lower, mid, NT) + dot(lower, low, NT)
    last = cum_t[pos - 1 : pos, :]
    trail_t = jnp.exp(last - cum_t)
    for h in range(heads):
        trailb[h] = jnp.broadcast_to(trail_t[:, h : h + 1], (pos, DH))
    my_row = totals.at[c // 8, c % 8]
    my_row[...] = last

    loads[1].wait()
    loads[2].wait()

    def own_state(h):
        keys = (k[:, lanes(h)].astype(F32) * trailb[h]).astype(BF16)
        dk[:, lanes(h)] = keys
        state = dot(keys, v[:, lanes(h)], TN).astype(BF16)
        s_send[shares(h)] = state.reshape(per_head, rows, DH)

    for group in range(len(groups)):
        each(group * group_heads, (group + 1) * group_heads, own_state, 2)
        if group == 0:
            pl.semaphore_wait(barrier, n)
            for i in range(1, 8):
                pltpu.make_async_remote_copy(
                    src_ref=my_row, dst_ref=my_row,
                    send_sem=sum_sem.at[2], recv_sem=sum_sem.at[3],
                    device_id=((c // 8) * 8 + (c + i) % 8, core), device_id_type=MESH,
                ).start()
        to_owners(s_send, s_recv, 0, group)

    cum_h = dot(hi, lower, NT) + dot(mid, lower, NT) + dot(low, lower, NT)
    cum[...] = cum_h[:heads]
    lead_t = jnp.exp(cum_t)
    for h in range(heads):
        cumb[h] = jnp.broadcast_to(cum_t[:, h : h + 1], (pos, DH))
        leadb[h] = jnp.broadcast_to(lead_t[:, h : h + 1], (pos, DH))

    loads[3].wait()

    def inside(h):
        scores = dot(q[:, lanes(h)], k[:, lanes(h)], NT)
        row = cum[pl.ds(h, 1), :]
        col = cumb[h]
        spread = jnp.concatenate([col, col], axis=1) - row
        d = jnp.exp(jnp.where(t_i >= s_i, spread, -1e30))
        decay[h] = d
        w = (scores * d).astype(BF16)
        weights[h] = w
        attn[:, lanes(h)] = dot(w, v[:, lanes(h)], NN)
        lead_q = (q[:, lanes(h)].astype(F32) * leadb[h]).astype(BF16)
        ql[:, lanes(h)] = lead_q
        qt[h] = lead_q.T

    each(0, heads // 4, inside, 2)

    any_copy(totals.at[0, pl.ds(0, 7)], sum_sem.at[2], sum_sem.at[3]).wait()
    for i in range(1, 8):
        pltpu.make_async_remote_copy(
            src_ref=totals.at[c // 8], dst_ref=totals.at[c // 8],
            send_sem=sum_sem.at[4], recv_sem=sum_sem.at[5],
            device_id=((c // 8 + i) % 8 * 8 + c % 8, core), device_id_type=MESH,
        ).start()

    each(heads // 4, heads // 2, inside, 2)

    any_copy(totals.at[pl.ds(0, 7)], sum_sem.at[4], sum_sem.at[5]).wait()
    every = totals[...].reshape(n, DH)
    lane_i = lax.broadcasted_iota(jnp.int32, (n, DH), 1)
    total = jnp.sum(jnp.where(lane_i == mine // per_head, every, 0.0), axis=1, keepdims=True)
    block_decay[...] = jnp.broadcast_to(jnp.exp(total), (n, DH))

    def scan(src, dst, reverse):
        def one(i, state):
            j = n - 1 - i if reverse else i
            dst[j] = state.astype(BF16)
            return state * block_decay[pl.ds(j, 1), :] + src[j].astype(F32)

        lax.fori_loop(0, n, one, jnp.zeros((rows, DH), F32), unroll=8)

    owners_wait(s_recv, 0)
    scan(s_recv, e_send, False)
    from_owner(e_send, e_recv, 0)

    each(heads // 2, heads, inside, 2)
    loads[4].wait()
    loads[5].wait()

    def prepare(h):
        gg[:, lanes(h)] = gain[:, lanes(h)] * g[:, lanes(h)].astype(F32)
        dv[:, lanes(h)] = (v[:, lanes(h)].astype(F32) * trailb[h]).astype(BF16)

    each(0, heads, prepare, 2)

    def attend(h, carry):
        squares, inner = carry
        entering = e_recv[shares(h)].reshape(DH, DH)
        a = attn[:, lanes(h)] + dot(ql[:, lanes(h)], entering, NN)
        attn[:, lanes(h)] = a
        return squares + a * a, inner + a * gg[:, lanes(h)]

    squares = inner = jnp.zeros((pos, DH), F32)
    for group in range(len(groups)):
        group_wait(e_recv, 0, group)
        squares, inner = lax.fori_loop(
            group * group_heads, (group + 1) * group_heads, attend, (squares, inner), unroll=2
        )
    squares = jnp.sum(squares, axis=1, keepdims=True)
    inner = jnp.sum(inner, axis=1, keepdims=True)
    half_i = lax.broadcasted_iota(jnp.int32, (pos, DH), 1)
    sums[...] = jnp.where(half_i < DH // 2, squares, inner)
    swap = pltpu.make_async_remote_copy(
        src_ref=sums, dst_ref=sums_in, send_sem=sum_sem.at[0], recv_sem=sum_sem.at[1],
        device_id=(c, 1 - core), device_id_type=MESH,
    )
    swap.start()
    swap.wait()
    both = sums[...] + sums_in[...]
    full = 2 * width
    scale = lax.rsqrt(both[:, 0:1] / full + EPSILON)
    pull = scale * scale * scale * (both[:, DH - 1 : DH] / full)
    sums[...] = jnp.broadcast_to(scale, (pos, DH))
    sums_in[...] = jnp.broadcast_to(pull, (pos, DH))

    def own_grad(h):
        d = (sums[...] * gg[:, lanes(h)] - attn[:, lanes(h)] * sums_in[...]).astype(BF16)
        d_attn[:, lanes(h)] = d
        state = dot(qt[h], d, NN).astype(BF16)
        t_send[shares(h)] = state.reshape(per_head, rows, DH)

    for group in range(len(groups)):
        each(group * group_heads, (group + 1) * group_heads, own_grad, 2)
        to_owners(t_send, t_recv, 1, group)

    def gradients(h):
        d = d_attn[:, lanes(h)]
        out[:, lanes(h)] = (attn[:, lanes(h)] * sums[...] * gain[:, lanes(h)]).astype(BF16)
        w = weights[h]
        gw = (dot(d, v[:, lanes(h)], NT) * decay[h]).astype(BF16)
        entering = e_recv[shares(h)].reshape(DH, DH)
        gq[:, lanes(h)] = (
            leadb[h] * dot(d, entering, NT) + dot(gw, k[:, lanes(h)], NN)
        ).astype(BF16)
        attn[:, lanes(h)] = dot(gw, q[:, lanes(h)], TN)
        decay[h, :, 0:DH] = dot(w, d, TN)

    each(0, heads // 2, gradients, 1)
    owners_wait(t_recv, 1)
    scan(t_recv, l_send, True)
    from_owner(l_send, l_recv, 1)
    each(heads // 2, heads, gradients, 1)

    def finish(h):
        leaving = l_recv[shares(h)].reshape(DH, DH)
        gk[:, lanes(h)] = (attn[:, lanes(h)] + dot(dv[:, lanes(h)], leaving, NT)).astype(BF16)
        gv[:, lanes(h)] = (decay[h, :, 0:DH] + dot(dk[:, lanes(h)], leaving, NN)).astype(BF16)

    for group in range(len(groups)):
        group_wait(l_recv, 1, group)
        each(group * group_heads, (group + 1) * group_heads, finish, 2)

    for which, ref in enumerate((s_send, t_send, e_send, l_send)):
        any_copy(ref.at[pl.ds(0, n - 1)], share_sem.at[(0, 2, 4, 5)[which]], share_sem.at[1]).wait_send()


def write_out(*refs):
    copies = [
        pltpu.make_async_copy(src, dst, refs[8].at[i])
        for i, (src, dst) in enumerate(zip(refs[:4], refs[4:8]))
    ]
    for copy in copies:
        copy.start()
    for copy in copies:
        copy.wait()


def solution(mesh):
    n = mesh.shape["ctx"]

    def local(queries, keys, values, log_decay, norm_gain, d_out):
        pos, width = queries.shape
        heads = width // DH
        rows = DH * heads // n
        wide = jax.ShapeDtypeStruct((pos, width), BF16)
        hbm = pl.BlockSpec(memory_space=pltpu.HBM)
        vmem = pl.BlockSpec(memory_space=pltpu.VMEM)
        shares = pltpu.VMEM((n, rows, DH), BF16)
        columns = pltpu.VMEM((heads, pos, DH), F32)
        flat = pltpu.VMEM((pos, width), BF16)
        flat_f32 = pltpu.VMEM((pos, width), F32)
        small = pltpu.VMEM((pos, DH), F32)
        held = pl.pallas_call(
            functools.partial(kernel, n, heads, pos),
            out_shape=[pltpu.VMEM((pos, width), BF16)] * 4,
            in_specs=[hbm] * 6,
            out_specs=[vmem] * 4,
            scratch_shapes=[
                flat, flat, flat, flat,
                pltpu.VMEM((heads, pos), F32),
                pltpu.VMEM((1, width), F32),
                pltpu.VMEM((heads, pos), F32),
                columns, columns, columns,
                pltpu.VMEM((heads, pos, pos), F32),
                pltpu.VMEM((heads, pos, pos), BF16),
                flat, flat, flat,
                pltpu.VMEM((heads, DH, pos), BF16),
                flat_f32, flat_f32, flat,
                shares, shares, shares, shares, shares, shares, shares, shares,
                pltpu.VMEM((8, n // 8, 1, DH), F32),
                pltpu.VMEM((n, DH), F32),
                small, small,
                pltpu.SemaphoreType.DMA((6,)),
                pltpu.SemaphoreType.DMA((6,)),
                pltpu.SemaphoreType.DMA((2, SPLIT[0] * SPLIT[1] * SPLIT[2])),
                pltpu.SemaphoreType.DMA((6,)),
            ],
            compiler_params=pltpu.CompilerParams(
                collective_id=0, has_side_effects=True, vmem_limit_bytes=44 * 2**20
            ),
            cost_estimate=pl.CostEstimate(
                flops=36 * pos * DH * DH * heads, bytes_accessed=16 * pos * width, transcendentals=0
            ),
            name="attention",
        )(*(pltpu.with_memory_space_constraint(a, pltpu.HBM) for a in (queries, keys, values, log_decay, norm_gain.reshape(1, width), d_out)))
        return pl.pallas_call(
            write_out,
            out_shape=[wide] * 4,
            in_specs=[pl.BlockSpec(memory_space=pl.ANY)] * 4,
            out_specs=[hbm] * 4,
            scratch_shapes=[pltpu.SemaphoreType.DMA((4,))],
            compiler_params=pltpu.CompilerParams(vmem_limit_bytes=16 * 2**20),
            name="write_out",
        )(*(pltpu.with_memory_space_constraint(a, pltpu.VMEM) for a in held))

    wide = P("ctx", "head")
    return jax.shard_map(
        local,
        mesh=mesh,
        in_specs=(wide, wide, wide, P("head", "ctx"), P("head"), wide),
        out_specs=(wide, wide, wide, wide),
        check_vma=False,
    )
```

```python
import functools
import itertools

import jax
import jax.numpy as jnp
from jax import lax
from jax.experimental import pallas as pl
from jax.experimental.pallas import tpu as pltpu
from jax.sharding import PartitionSpec as P

DH = 128
EPSILON = 1e-06
SIDE = 4
SPLIT = (1, 2, 2)
HOPS = (0, 1, 2, 1)
MESH = pl.DeviceIdType.MESH
F32 = jnp.float32
BF16 = jnp.bfloat16
NN = ((1,), (0,))
NT = ((1,), (1,))
TN = ((0,), (0,))


def dot(a, b, dims):
    return lax.dot_general(a, b, (dims, ((), ())), preferred_element_type=F32)


def routes(place, group, split):
    per_axis = []
    for at, chosen, part in zip(place, group, split):
        steps = []
        for turn in range(SIDE // part):
            shift = (chosen - at) % part + part * turn
            hops = sum(HOPS[part * turn + i] for i in range(part)) / part
            steps.append(((at + shift) % SIDE, hops, turn == 0))
        per_axis.append(steps)
    found = []
    for steps in itertools.product(*per_axis):
        ctx, member = 0, 0
        for (at, _, _), part in zip(steps, split):
            ctx = ctx * SIDE + at
            member = member * (SIDE // part) + at // part
        found.append((sum(s[1] for s in steps), ctx, member, all(s[2] for s in steps)))
    found.sort(key=lambda r: -r[0])
    return [r[1:] for r in found]


def parts_of(a):
    hi = a.astype(BF16)
    rest = a - hi.astype(F32)
    mid = rest.astype(BF16)
    return [hi, mid, (rest - mid.astype(F32)).astype(BF16)]


def along_lanes(a):
    ones = jnp.ones((8, a.shape[1]), BF16)
    return sum(dot(ones, part, NT) for part in parts_of(a))


def kernel(
    n, heads, pos,
    q_hbm, k_hbm, v_hbm, ld_hbm, gain_hbm, g_hbm,
    out, gq, gk, gv,
    q, k, v, g, ld, gain,
    cum, trail_h, kt, cumb, leadb, trailb, decay, weights, dk, dv, ql, qt,
    attn, gg, d_attn,
    s_send, s_recv, e_send, e_recv, t_send, t_recv, l_send, l_recv,
    totals, block_decay, sums, sums_in, scaleb, pullb,
    in_sem, share_sem, group_sem, sum_sem,
):
    c = lax.axis_index("ctx")
    core = lax.axis_index("head")
    place = (c // (SIDE * SIDE), (c // SIDE) % SIDE, c % SIDE)
    rows = DH * heads // n
    per_head = n // heads
    groups = list(itertools.product(*(range(part) for part in SPLIT)))
    members = n // len(groups)
    group_heads = heads // len(groups)
    my_group, my_member = 0, 0
    for at, part in zip(place, SPLIT):
        my_group = my_group * part + at % part
        my_member = my_member * (SIDE // part) + at // part
    mine = my_group * members + my_member
    width = heads * DH

    loads = [
        pltpu.make_async_copy(src, dst, in_sem.at[i])
        for i, (src, dst) in enumerate(
            ((ld_hbm, ld), (k_hbm, k), (v_hbm, v), (q_hbm, q), (gain_hbm, gain), (g_hbm, g))
        )
    ]
    for load in loads:
        load.start()

    barrier = pltpu.get_barrier_semaphore()

    def greet(i, _):
        pl.semaphore_signal(
            barrier, inc=1, device_id=((c + i) % n, core), device_id_type=MESH
        )
        return 0

    lax.fori_loop(1, n, greet, 0)
    pl.semaphore_signal(barrier, inc=1, device_id=(c, 1 - core), device_id_type=MESH)

    def lanes(h):
        return pl.ds(h * DH, DH) if isinstance(h, int) else pl.ds(pl.multiple_of(h * DH, DH), DH)

    def shares(h):
        return pl.ds(h * per_head, per_head)

    def send(src, dst, sent, landed, dest, maybe_me):
        def away():
            pltpu.make_async_remote_copy(
                src_ref=src, dst_ref=dst, send_sem=sent, recv_sem=landed,
                device_id=(dest, core), device_id_type=MESH,
            ).start()

        if maybe_me:
            pl.when(dest != c)(away)

            @pl.when(dest == c)
            def _():
                pltpu.make_async_copy(src, dst, landed).start()
        else:
            away()

    def to_owners(src, dst, which, group):
        for dest, member, maybe_me in routes(place, groups[group], SPLIT):
            send(
                src.at[group * members + member], dst.at[c],
                share_sem.at[2 * which], share_sem.at[2 * which + 1], dest, maybe_me,
            )

    def from_owner(src, dst, which):
        for dest, _, maybe_me in routes(place, (0, 0, 0), (1, 1, 1)):
            send(
                src.at[dest], dst.at[mine],
                share_sem.at[4 + which], group_sem.at[which, my_group], dest, maybe_me,
            )

    def any_copy(ref, sent, landed):
        return pltpu.make_async_remote_copy(
            src_ref=ref, dst_ref=ref, send_sem=sent, recv_sem=landed,
            device_id=((c + 1) % n, core), device_id_type=MESH,
        )

    def owners_wait(dst, which):
        any_copy(dst, share_sem.at[2 * which], share_sem.at[2 * which + 1]).wait_recv()

    def group_wait(dst, which, group):
        any_copy(
            dst.at[pl.ds(group * members, members)],
            share_sem.at[4 + which], group_sem.at[which, group],
        ).wait_recv()

    def each(first, last, body, unroll):
        def step(h, _):
            body(h)
            return 0

        lax.fori_loop(first, last, step, 0, unroll=unroll)

    t_i = lax.broadcasted_iota(jnp.int32, (pos, pos), 0)
    s_i = lax.broadcasted_iota(jnp.int32, (pos, pos), 1)
    lower = jnp.where(t_i >= s_i, 1.0, 0.0).astype(BF16)

    loads[0].wait()
    ld_all = ld[...]
    hi = ld_all.astype(BF16)
    rest = ld_all - hi.astype(F32)
    mid = rest.astype(BF16)
    low = (rest - mid.astype(F32)).astype(BF16)
    parts = jnp.concatenate([hi, mid, low], axis=0)
    summed = dot(parts, lower, NT)
    cum_h = summed[:heads] + summed[heads : 2 * heads] + summed[2 * heads :]
    cum[...] = cum_h
    trail_h[...] = jnp.exp(cum_h[:, pos - 1 :] - cum_h)
    my_row = totals.at[c // 8, c % 8]
    padded = jnp.concatenate([cum_h[:, pos - DH :], jnp.zeros((DH - heads, DH), F32)], axis=0)
    my_row[...] = padded.T[DH - 1 :, :]

    loads[1].wait()

    def turn(h):
        kt[h] = k[:, lanes(h)].T

    each(0, heads, turn, 4)
    loads[2].wait()

    def own_state(h):
        keys = (kt[h].astype(F32) * trail_h[pl.ds(h, 1), :]).astype(BF16)
        state = dot(keys, v[:, lanes(h)], NN).astype(BF16)
        s_send[shares(h)] = state.reshape(per_head, rows, DH)

    def send_totals():
        for i in range(1, 8):
            pltpu.make_async_remote_copy(
                src_ref=my_row, dst_ref=my_row,
                send_sem=sum_sem.at[2], recv_sem=sum_sem.at[3],
                device_id=((c // 8) * 8 + (c + i) % 8, core), device_id_type=MESH,
            ).start()

    each(0, heads, own_state, 4)
    pl.semaphore_wait(barrier, n)
    send_totals()
    for group in range(len(groups)):
        to_owners(s_send, s_recv, 0, group)

    parts = jnp.concatenate([parts, jnp.zeros((DH - 3 * heads, pos), BF16)], axis=0)
    summed = dot(lower, parts, NT)
    cum_t = summed[:, :heads] + summed[:, heads : 2 * heads] + summed[:, 2 * heads : 3 * heads]
    trail_t = jnp.exp(cum_t[pos - 1 :, :] - cum_t)
    lead_t = jnp.exp(cum_t)
    for h in range(heads):
        cumb[h] = jnp.broadcast_to(cum_t[:, h : h + 1], (pos, DH))
        leadb[h] = jnp.broadcast_to(lead_t[:, h : h + 1], (pos, DH))
        trailb[h] = jnp.broadcast_to(trail_t[:, h : h + 1], (pos, DH))

    loads[3].wait()

    def inside(h):
        scores = dot(q[:, lanes(h)], k[:, lanes(h)], NT)
        row = cum[pl.ds(h, 1), :]
        col = cumb[h]
        spread = jnp.concatenate([col, col], axis=1) - row
        d = jnp.exp(jnp.where(t_i >= s_i, spread, -1e30))
        decay[h] = d
        w = (scores * d).astype(BF16)
        weights[h] = w
        attn[:, lanes(h)] = dot(w, v[:, lanes(h)], NN)
        lead_q = (q[:, lanes(h)].astype(F32) * leadb[h]).astype(BF16)
        ql[:, lanes(h)] = lead_q
        qt[h] = lead_q.T

    each(0, heads // 4, inside, 2)

    any_copy(totals.at[0, pl.ds(0, 7)], sum_sem.at[2], sum_sem.at[3]).wait()
    for i in range(1, 8):
        pltpu.make_async_remote_copy(
            src_ref=totals.at[c // 8], dst_ref=totals.at[c // 8],
            send_sem=sum_sem.at[4], recv_sem=sum_sem.at[5],
            device_id=((c // 8 + i) % 8 * 8 + c % 8, core), device_id_type=MESH,
        ).start()

    each(heads // 4, heads // 2, inside, 2)

    any_copy(totals.at[pl.ds(0, 7)], sum_sem.at[4], sum_sem.at[5]).wait()
    every = totals[...].reshape(n, DH)
    lane_i = lax.broadcasted_iota(jnp.int32, (n, DH), 1)
    total = jnp.sum(jnp.where(lane_i == mine // per_head, every, 0.0), axis=1, keepdims=True)
    block_decay[...] = jnp.broadcast_to(jnp.exp(total), (n, DH))

    def scan(src, dst, reverse):
        def one(i, state):
            j = n - 1 - i if reverse else i
            dst[j] = state.astype(BF16)
            return state * block_decay[pl.ds(j, 1), :] + src[j].astype(F32)

        lax.fori_loop(0, n, one, jnp.zeros((rows, DH), F32), unroll=8)

    owners_wait(s_recv, 0)
    scan(s_recv, e_send, False)
    from_owner(e_send, e_recv, 0)

    each(heads // 2, heads, inside, 2)
    loads[4].wait()
    loads[5].wait()

    def prepare(h):
        gg[:, lanes(h)] = gain[:, lanes(h)] * g[:, lanes(h)].astype(F32)
        dk[:, lanes(h)] = (k[:, lanes(h)].astype(F32) * trailb[h]).astype(BF16)
        dv[:, lanes(h)] = (v[:, lanes(h)].astype(F32) * trailb[h]).astype(BF16)

    each(0, heads, prepare, 2)

    def attend(h, carry):
        squares, inner = carry
        entering = e_recv[shares(h)].reshape(DH, DH)
        a = attn[:, lanes(h)] + dot(ql[:, lanes(h)], entering, NN)
        attn[:, lanes(h)] = a
        return squares + a * a, inner + a * gg[:, lanes(h)]

    squares = inner = jnp.zeros((pos, DH), F32)
    for group in range(len(groups)):
        group_wait(e_recv, 0, group)
        squares, inner = lax.fori_loop(
            group * group_heads, (group + 1) * group_heads, attend, (squares, inner), unroll=4
        )
    sums[...] = jnp.concatenate([along_lanes(squares), along_lanes(inner)], axis=0)
    swap = pltpu.make_async_remote_copy(
        src_ref=sums, dst_ref=sums_in, send_sem=sum_sem.at[0], recv_sem=sum_sem.at[1],
        device_id=(c, 1 - core), device_id_type=MESH,
    )
    swap.start()
    swap.wait()
    both = (sums[...] + sums_in[...]) / (2 * width)
    scale = lax.rsqrt(both[:8] + EPSILON)
    pull = scale * scale * scale * both[8:]
    part_i = lax.broadcasted_iota(jnp.int32, (48, 2 * DH), 0)
    lane_i = lax.broadcasted_iota(jnp.int32, (48, 2 * DH), 1)
    chosen = (part_i % 8 == 0) & ((part_i < 24) == (lane_i < DH))
    both = dot(
        jnp.concatenate(parts_of(scale) + parts_of(pull), axis=0),
        jnp.where(chosen, 1.0, 0.0).astype(BF16), TN,
    )
    scaleb[...] = both[:, :DH]
    pullb[...] = both[:, DH:]

    def own_grad(h):
        d = (scaleb[...] * gg[:, lanes(h)] - attn[:, lanes(h)] * pullb[...]).astype(BF16)
        d_attn[:, lanes(h)] = d
        state = dot(qt[h], d, NN).astype(BF16)
        t_send[shares(h)] = state.reshape(per_head, rows, DH)

    for group in range(len(groups)):
        each(group * group_heads, (group + 1) * group_heads, own_grad, 4)
        to_owners(t_send, t_recv, 1, group)

    def gradients(h):
        d = d_attn[:, lanes(h)]
        out[:, lanes(h)] = (attn[:, lanes(h)] * scaleb[...] * gain[:, lanes(h)]).astype(BF16)
        w = weights[h]
        gw = (dot(d, v[:, lanes(h)], NT) * decay[h]).astype(BF16)
        entering = e_recv[shares(h)].reshape(DH, DH)
        gq[:, lanes(h)] = (
            leadb[h] * dot(d, entering, NT) + dot(gw, k[:, lanes(h)], NN)
        ).astype(BF16)
        attn[:, lanes(h)] = dot(gw, q[:, lanes(h)], TN)
        decay[h, :, 0:DH] = dot(w, d, TN)

    each(0, heads // 2, gradients, 1)
    owners_wait(t_recv, 1)
    scan(t_recv, l_send, True)
    from_owner(l_send, l_recv, 1)
    each(heads // 2, heads, gradients, 1)

    def finish(h):
        leaving = l_recv[shares(h)].reshape(DH, DH)
        gk[:, lanes(h)] = (attn[:, lanes(h)] + dot(dv[:, lanes(h)], leaving, NT)).astype(BF16)
        gv[:, lanes(h)] = (decay[h, :, 0:DH] + dot(dk[:, lanes(h)], leaving, NN)).astype(BF16)

    for group in range(len(groups)):
        group_wait(l_recv, 1, group)
        each(group * group_heads, (group + 1) * group_heads, finish, 4)

    for which, ref in enumerate((s_send, t_send, e_send, l_send)):
        any_copy(ref.at[pl.ds(0, n - 1)], share_sem.at[(0, 2, 4, 5)[which]], share_sem.at[1]).wait_send()


def write_out(*refs):
    copies = [
        pltpu.make_async_copy(src, dst, refs[8].at[i])
        for i, (src, dst) in enumerate(zip(refs[:4], refs[4:8]))
    ]
    for copy in copies:
        copy.start()
    for copy in copies:
        copy.wait()


def solution(mesh):
    n = mesh.shape["ctx"]

    def local(queries, keys, values, log_decay, norm_gain, d_out):
        pos, width = queries.shape
        heads = width // DH
        rows = DH * heads // n
        wide = jax.ShapeDtypeStruct((pos, width), BF16)
        hbm = pl.BlockSpec(memory_space=pltpu.HBM)
        vmem = pl.BlockSpec(memory_space=pltpu.VMEM)
        shares = pltpu.VMEM((n, rows, DH), BF16)
        columns = pltpu.VMEM((heads, pos, DH), F32)
        flat = pltpu.VMEM((pos, width), BF16)
        flat_f32 = pltpu.VMEM((pos, width), F32)
        small = pltpu.VMEM((pos, DH), F32)
        held = pl.pallas_call(
            functools.partial(kernel, n, heads, pos),
            out_shape=[pltpu.VMEM((pos, width), BF16)] * 4,
            in_specs=[hbm] * 6,
            out_specs=[vmem] * 4,
            scratch_shapes=[
                flat, flat, flat, flat,
                pltpu.VMEM((heads, pos), F32),
                pltpu.VMEM((1, width), F32),
                pltpu.VMEM((heads, pos), F32),
                pltpu.VMEM((heads, pos), F32),
                pltpu.VMEM((heads, DH, pos), BF16),
                columns, columns, columns,
                pltpu.VMEM((heads, pos, pos), F32),
                pltpu.VMEM((heads, pos, pos), BF16),
                flat, flat, flat,
                pltpu.VMEM((heads, DH, pos), BF16),
                flat_f32, flat_f32, flat,
                shares, shares, shares, shares, shares, shares, shares, shares,
                pltpu.VMEM((8, n // 8, 1, DH), F32),
                pltpu.VMEM((n, DH), F32),
                pltpu.VMEM((16, pos), F32),
                pltpu.VMEM((16, pos), F32),
                small, small,
                pltpu.SemaphoreType.DMA((6,)),
                pltpu.SemaphoreType.DMA((6,)),
                pltpu.SemaphoreType.DMA((2, SPLIT[0] * SPLIT[1] * SPLIT[2])),
                pltpu.SemaphoreType.DMA((6,)),
            ],
            compiler_params=pltpu.CompilerParams(
                collective_id=0, has_side_effects=True, vmem_limit_bytes=44 * 2**20
            ),
            cost_estimate=pl.CostEstimate(
                flops=36 * pos * DH * DH * heads, bytes_accessed=16 * pos * width, transcendentals=0
            ),
            name="attention",
        )(*(pltpu.with_memory_space_constraint(a, pltpu.HBM) for a in (queries, keys, values, log_decay, norm_gain.reshape(1, width), d_out)))
        return pl.pallas_call(
            write_out,
            out_shape=[wide] * 4,
            in_specs=[pl.BlockSpec(memory_space=pl.ANY)] * 4,
            out_specs=[hbm] * 4,
            scratch_shapes=[pltpu.SemaphoreType.DMA((4,))],
            compiler_params=pltpu.CompilerParams(vmem_limit_bytes=16 * 2**20),
            name="write_out",
        )(*(pltpu.with_memory_space_constraint(a, pltpu.VMEM) for a in held))

    wide = P("ctx", "head")
    return jax.shard_map(
        local,
        mesh=mesh,
        in_specs=(wide, wide, wide, P("head", "ctx"), P("head"), wide),
        out_specs=(wide, wide, wide, wide),
        check_vma=False,
    )
```

```python
import functools
import itertools

import jax
import jax.numpy as jnp
from jax import lax
from jax.experimental import pallas as pl
from jax.experimental.pallas import tpu as pltpu
from jax.sharding import PartitionSpec as P

DH = 128
EPSILON = 1e-06
SIDE = 4
SPLIT = (1, 2, 2)
PAIR = 2
HOPS = (0, 1, 2, 1)
MESH = pl.DeviceIdType.MESH
F32 = jnp.float32
BF16 = jnp.bfloat16
NN = ((1,), (0,))
NT = ((1,), (1,))
TN = ((0,), (0,))


def dot(a, b, dims):
    return lax.dot_general(a, b, (dims, ((), ())), preferred_element_type=F32)


def routes(place, group, split):
    per_axis = []
    for at, chosen, part in zip(place, group, split):
        steps = []
        for turn in range(SIDE // part):
            shift = (chosen - at) % part + part * turn
            hops = sum(HOPS[part * turn + i] for i in range(part)) / part
            steps.append(((at + shift) % SIDE, hops, turn == 0))
        per_axis.append(steps)
    found = []
    for steps in itertools.product(*per_axis):
        ctx, member = 0, 0
        for (at, _, _), part in zip(steps, split):
            ctx = ctx * SIDE + at
            member = member * (SIDE // part) + at // part
        found.append((sum(s[1] for s in steps), ctx, member, all(s[2] for s in steps)))
    found.sort(key=lambda r: -r[0])
    return [r[1:] for r in found]


def parts_of(a):
    hi = a.astype(BF16)
    rest = a - hi.astype(F32)
    mid = rest.astype(BF16)
    return [hi, mid, (rest - mid.astype(F32)).astype(BF16)]


def along_lanes(a):
    ones = jnp.ones((8, a.shape[1]), BF16)
    return sum(dot(ones, part, NT) for part in parts_of(a))


def kernel(
    n, heads, pos,
    q_hbm, k_hbm, v_hbm, ld_hbm, gain_hbm, g_hbm,
    out, gq, gk, gv,
    q, k, v, g, ld, gain,
    cum, trail_h, kt, cumb, leadb, trailb, decay, weights, dk, dv, ql, qt,
    attn, gg, d_attn,
    s_send, s_recv, e_send, e_recv, t_send, t_recv, l_send, l_recv,
    totals, block_decay, sums, sums_in, scaleb, pullb,
    in_sem, share_sem, group_sem, sum_sem,
):
    c = lax.axis_index("ctx")
    core = lax.axis_index("head")
    place = (c // (SIDE * SIDE), (c // SIDE) % SIDE, c % SIDE)
    rows = DH * heads // n
    per_head = n // heads
    groups = list(itertools.product(*(range(part) for part in SPLIT)))
    members = n // len(groups)
    group_heads = heads // len(groups)
    my_group, my_member = 0, 0
    for at, part in zip(place, SPLIT):
        my_group = my_group * part + at % part
        my_member = my_member * (SIDE // part) + at // part
    mine = my_group * members + my_member
    width = heads * DH

    loads = [
        pltpu.make_async_copy(src, dst, in_sem.at[i])
        for i, (src, dst) in enumerate(
            ((ld_hbm, ld), (k_hbm, k), (v_hbm, v), (q_hbm, q), (gain_hbm, gain), (g_hbm, g))
        )
    ]
    for load in loads:
        load.start()

    barrier = pltpu.get_barrier_semaphore()

    def greet(i, _):
        pl.semaphore_signal(
            barrier, inc=1, device_id=((c + i) % n, core), device_id_type=MESH
        )
        return 0

    lax.fori_loop(1, n, greet, 0)
    pl.semaphore_signal(barrier, inc=1, device_id=(c, 1 - core), device_id_type=MESH)

    def lanes(h):
        return pl.ds(h * DH, DH) if isinstance(h, int) else pl.ds(pl.multiple_of(h * DH, DH), DH)

    def shares(h):
        return pl.ds(h * per_head, per_head)

    def send(src, dst, sent, landed, dest, maybe_me):
        def away():
            pltpu.make_async_remote_copy(
                src_ref=src, dst_ref=dst, send_sem=sent, recv_sem=landed,
                device_id=(dest, core), device_id_type=MESH,
            ).start()

        if maybe_me:
            pl.when(dest != c)(away)

            @pl.when(dest == c)
            def _():
                pltpu.make_async_copy(src, dst, landed).start()
        else:
            away()

    def to_owners(src, dst, which, group):
        for dest, member, maybe_me in routes(place, groups[group], SPLIT):
            send(
                src.at[group * members + member], dst.at[c],
                share_sem.at[2 * which], share_sem.at[2 * which + 1], dest, maybe_me,
            )

    def from_owner(src, dst, which):
        for dest, _, maybe_me in routes(place, (0, 0, 0), (1, 1, 1)):
            send(
                src.at[dest], dst.at[mine],
                share_sem.at[4 + which], group_sem.at[which, my_group], dest, maybe_me,
            )

    def any_copy(ref, sent, landed):
        return pltpu.make_async_remote_copy(
            src_ref=ref, dst_ref=ref, send_sem=sent, recv_sem=landed,
            device_id=((c + 1) % n, core), device_id_type=MESH,
        )

    def owners_wait(dst, which):
        any_copy(dst, share_sem.at[2 * which], share_sem.at[2 * which + 1]).wait_recv()

    def group_wait(dst, which, group):
        any_copy(
            dst.at[pl.ds(group * members, members)],
            share_sem.at[4 + which], group_sem.at[which, group],
        ).wait_recv()

    def each(first, last, body, unroll):
        def step(h, _):
            body(h)
            return 0

        lax.fori_loop(first, last, step, 0, unroll=unroll)

    t_i = lax.broadcasted_iota(jnp.int32, (pos, pos), 0)
    s_i = lax.broadcasted_iota(jnp.int32, (pos, pos), 1)
    lower = jnp.where(t_i >= s_i, 1.0, 0.0).astype(BF16)

    loads[0].wait()
    ld_all = ld[...]
    hi = ld_all.astype(BF16)
    rest = ld_all - hi.astype(F32)
    mid = rest.astype(BF16)
    low = (rest - mid.astype(F32)).astype(BF16)
    parts = jnp.concatenate([hi, mid, low], axis=0)
    summed = dot(parts, lower, NT)
    cum_h = summed[:heads] + summed[heads : 2 * heads] + summed[2 * heads :]
    cum[...] = cum_h
    trail_h[...] = jnp.exp(cum_h[:, pos - 1 :] - cum_h)
    my_row = totals.at[c // 8, c % 8]
    padded = jnp.concatenate([cum_h[:, pos - DH :], jnp.zeros((DH - heads, DH), F32)], axis=0)
    my_row[...] = padded.T[DH - 1 :, :]

    loads[1].wait()

    def turn(h):
        kt[h] = k[:, lanes(h)].T

    each(0, heads, turn, 4)
    loads[2].wait()

    def own_state(h):
        keys = (kt[h].astype(F32) * trail_h[pl.ds(h, 1), :]).astype(BF16)
        state = dot(keys, v[:, lanes(h)], NN).astype(BF16)
        s_send[shares(h)] = state.reshape(per_head, rows, DH)

    def send_totals():
        for i in range(1, 8):
            pltpu.make_async_remote_copy(
                src_ref=my_row, dst_ref=my_row,
                send_sem=sum_sem.at[2], recv_sem=sum_sem.at[3],
                device_id=((c // 8) * 8 + (c + i) % 8, core), device_id_type=MESH,
            ).start()

    each(0, heads, own_state, 4)
    pl.semaphore_wait(barrier, n)
    send_totals()
    for group in range(len(groups)):
        to_owners(s_send, s_recv, 0, group)

    parts = jnp.concatenate([parts, jnp.zeros((DH - 3 * heads, pos), BF16)], axis=0)
    summed = dot(lower, parts, NT)
    cum_t = summed[:, :heads] + summed[:, heads : 2 * heads] + summed[:, 2 * heads : 3 * heads]
    trail_t = jnp.exp(cum_t[pos - 1 :, :] - cum_t)
    lead_t = jnp.exp(cum_t)
    for h in range(heads):
        cumb[h] = jnp.broadcast_to(cum_t[:, h : h + 1], (pos, DH))
        leadb[h] = jnp.broadcast_to(lead_t[:, h : h + 1], (pos, DH))
        trailb[h] = jnp.broadcast_to(trail_t[:, h : h + 1], (pos, DH))

    loads[3].wait()

    def inside(h):
        scores = dot(q[:, lanes(h)], k[:, lanes(h)], NT)
        row = cum[pl.ds(h, 1), :]
        col = cumb[h]
        spread = jnp.concatenate([col, col], axis=1) - row
        d = jnp.exp(jnp.where(t_i >= s_i, spread, -1e30))
        decay[h] = d
        w = (scores * d).astype(BF16)
        weights[h] = w
        attn[:, lanes(h)] = dot(w, v[:, lanes(h)], NN)
        lead_q = (q[:, lanes(h)].astype(F32) * leadb[h]).astype(BF16)
        ql[:, lanes(h)] = lead_q
        qt[h] = lead_q.T

    each(0, heads // 4, inside, 2)

    any_copy(totals.at[0, pl.ds(0, 7)], sum_sem.at[2], sum_sem.at[3]).wait()
    for i in range(1, 8):
        pltpu.make_async_remote_copy(
            src_ref=totals.at[c // 8], dst_ref=totals.at[c // 8],
            send_sem=sum_sem.at[4], recv_sem=sum_sem.at[5],
            device_id=((c // 8 + i) % 8 * 8 + c % 8, core), device_id_type=MESH,
        ).start()

    each(heads // 4, heads // 2, inside, 2)

    any_copy(totals.at[pl.ds(0, 7)], sum_sem.at[4], sum_sem.at[5]).wait()
    every = totals[...].reshape(n, DH)
    lane_i = lax.broadcasted_iota(jnp.int32, (n, DH), 1)
    total = jnp.sum(jnp.where(lane_i == mine // per_head, every, 0.0), axis=1, keepdims=True)
    block_decay[...] = jnp.broadcast_to(jnp.exp(total), (n, DH))

    def scan(src, dst, reverse):
        def one(i, state):
            j = n - 1 - i if reverse else i
            dst[j] = state.astype(BF16)
            return state * block_decay[pl.ds(j, 1), :] + src[j].astype(F32)

        lax.fori_loop(0, n, one, jnp.zeros((rows, DH), F32), unroll=8)

    owners_wait(s_recv, 0)
    scan(s_recv, e_send, False)
    from_owner(e_send, e_recv, 0)

    each(heads // 2, heads, inside, 2)
    loads[4].wait()
    loads[5].wait()

    def prepare(h):
        gg[:, lanes(h)] = gain[:, lanes(h)] * g[:, lanes(h)].astype(F32)
        dk[:, lanes(h)] = (k[:, lanes(h)].astype(F32) * trailb[h]).astype(BF16)
        dv[:, lanes(h)] = (v[:, lanes(h)].astype(F32) * trailb[h]).astype(BF16)

    each(0, heads, prepare, 2)

    def attend(h, carry):
        squares, inner = carry
        entering = e_recv[shares(h)].reshape(DH, DH)
        a = attn[:, lanes(h)] + dot(ql[:, lanes(h)], entering, NN)
        attn[:, lanes(h)] = a
        return squares + a * a, inner + a * gg[:, lanes(h)]

    squares = inner = jnp.zeros((pos, DH), F32)
    for group in range(0, len(groups), PAIR):
        for i in range(PAIR):
            group_wait(e_recv, 0, group + i)
        squares, inner = lax.fori_loop(
            group * group_heads, (group + PAIR) * group_heads, attend, (squares, inner),
            unroll=PAIR * group_heads,
        )
    sums[...] = jnp.concatenate([along_lanes(squares), along_lanes(inner)], axis=0)
    swap = pltpu.make_async_remote_copy(
        src_ref=sums, dst_ref=sums_in, send_sem=sum_sem.at[0], recv_sem=sum_sem.at[1],
        device_id=(c, 1 - core), device_id_type=MESH,
    )
    swap.start()
    swap.wait()
    both = (sums[...] + sums_in[...]) / (2 * width)
    scale = lax.rsqrt(both[:8] + EPSILON)
    pull = scale * scale * scale * both[8:]
    part_i = lax.broadcasted_iota(jnp.int32, (48, 2 * DH), 0)
    lane_i = lax.broadcasted_iota(jnp.int32, (48, 2 * DH), 1)
    chosen = (part_i % 8 == 0) & ((part_i < 24) == (lane_i < DH))
    both = dot(
        jnp.concatenate(parts_of(scale) + parts_of(pull), axis=0),
        jnp.where(chosen, 1.0, 0.0).astype(BF16), TN,
    )
    scaleb[...] = both[:, :DH]
    pullb[...] = both[:, DH:]

    def own_grad(h):
        d = (scaleb[...] * gg[:, lanes(h)] - attn[:, lanes(h)] * pullb[...]).astype(BF16)
        d_attn[:, lanes(h)] = d
        state = dot(qt[h], d, NN).astype(BF16)
        t_send[shares(h)] = state.reshape(per_head, rows, DH)

    for group in range(0, len(groups), PAIR):
        each(group * group_heads, (group + PAIR) * group_heads, own_grad, PAIR * group_heads)
        for i in range(PAIR):
            to_owners(t_send, t_recv, 1, group + i)

    def gradients(h):
        d = d_attn[:, lanes(h)]
        out[:, lanes(h)] = (attn[:, lanes(h)] * scaleb[...] * gain[:, lanes(h)]).astype(BF16)
        w = weights[h]
        gw = (dot(d, v[:, lanes(h)], NT) * decay[h]).astype(BF16)
        entering = e_recv[shares(h)].reshape(DH, DH)
        gq[:, lanes(h)] = (
            leadb[h] * dot(d, entering, NT) + dot(gw, k[:, lanes(h)], NN)
        ).astype(BF16)
        attn[:, lanes(h)] = dot(gw, q[:, lanes(h)], TN)
        decay[h, :, 0:DH] = dot(w, d, TN)

    each(0, heads // 2, gradients, 1)
    owners_wait(t_recv, 1)
    scan(t_recv, l_send, True)
    from_owner(l_send, l_recv, 1)
    each(heads // 2, heads, gradients, 1)

    def finish(h):
        leaving = l_recv[shares(h)].reshape(DH, DH)
        gk[:, lanes(h)] = (attn[:, lanes(h)] + dot(dv[:, lanes(h)], leaving, NT)).astype(BF16)
        gv[:, lanes(h)] = (decay[h, :, 0:DH] + dot(dk[:, lanes(h)], leaving, NN)).astype(BF16)

    for group in range(0, len(groups), PAIR):
        for i in range(PAIR):
            group_wait(l_recv, 1, group + i)
        each(group * group_heads, (group + PAIR) * group_heads, finish, PAIR * group_heads)

    for which, ref in enumerate((s_send, t_send, e_send, l_send)):
        any_copy(ref.at[pl.ds(0, n - 1)], share_sem.at[(0, 2, 4, 5)[which]], share_sem.at[1]).wait_send()


def write_out(*refs):
    copies = [
        pltpu.make_async_copy(src, dst, refs[8].at[i])
        for i, (src, dst) in enumerate(zip(refs[:4], refs[4:8]))
    ]
    for copy in copies:
        copy.start()
    for copy in copies:
        copy.wait()


def solution(mesh):
    n = mesh.shape["ctx"]

    def local(queries, keys, values, log_decay, norm_gain, d_out):
        pos, width = queries.shape
        heads = width // DH
        rows = DH * heads // n
        wide = jax.ShapeDtypeStruct((pos, width), BF16)
        hbm = pl.BlockSpec(memory_space=pltpu.HBM)
        vmem = pl.BlockSpec(memory_space=pltpu.VMEM)
        shares = pltpu.VMEM((n, rows, DH), BF16)
        columns = pltpu.VMEM((heads, pos, DH), F32)
        flat = pltpu.VMEM((pos, width), BF16)
        flat_f32 = pltpu.VMEM((pos, width), F32)
        small = pltpu.VMEM((pos, DH), F32)
        held = pl.pallas_call(
            functools.partial(kernel, n, heads, pos),
            out_shape=[pltpu.VMEM((pos, width), BF16)] * 4,
            in_specs=[hbm] * 6,
            out_specs=[vmem] * 4,
            scratch_shapes=[
                flat, flat, flat, flat,
                pltpu.VMEM((heads, pos), F32),
                pltpu.VMEM((1, width), F32),
                pltpu.VMEM((heads, pos), F32),
                pltpu.VMEM((heads, pos), F32),
                pltpu.VMEM((heads, DH, pos), BF16),
                columns, columns, columns,
                pltpu.VMEM((heads, pos, pos), F32),
                pltpu.VMEM((heads, pos, pos), BF16),
                flat, flat, flat,
                pltpu.VMEM((heads, DH, pos), BF16),
                flat_f32, flat_f32, flat,
                shares, shares, shares, shares, shares, shares, shares, shares,
                pltpu.VMEM((8, n // 8, 1, DH), F32),
                pltpu.VMEM((n, DH), F32),
                pltpu.VMEM((16, pos), F32),
                pltpu.VMEM((16, pos), F32),
                small, small,
                pltpu.SemaphoreType.DMA((6,)),
                pltpu.SemaphoreType.DMA((6,)),
                pltpu.SemaphoreType.DMA((2, SPLIT[0] * SPLIT[1] * SPLIT[2])),
                pltpu.SemaphoreType.DMA((6,)),
            ],
            compiler_params=pltpu.CompilerParams(
                collective_id=0, has_side_effects=True, vmem_limit_bytes=44 * 2**20
            ),
            cost_estimate=pl.CostEstimate(
                flops=36 * pos * DH * DH * heads, bytes_accessed=16 * pos * width, transcendentals=0
            ),
            name="attention",
        )(*(pltpu.with_memory_space_constraint(a, pltpu.HBM) for a in (queries, keys, values, log_decay, norm_gain.reshape(1, width), d_out)))
        return pl.pallas_call(
            write_out,
            out_shape=[wide] * 4,
            in_specs=[pl.BlockSpec(memory_space=pl.ANY)] * 4,
            out_specs=[hbm] * 4,
            scratch_shapes=[pltpu.SemaphoreType.DMA((4,))],
            compiler_params=pltpu.CompilerParams(vmem_limit_bytes=16 * 2**20),
            name="write_out",
        )(*(pltpu.with_memory_space_constraint(a, pltpu.VMEM) for a in held))

    wide = P("ctx", "head")
    return jax.shard_map(
        local,
        mesh=mesh,
        in_specs=(wide, wide, wide, P("head", "ctx"), P("head"), wide),
        out_specs=(wide, wide, wide, wide),
        check_vma=False,
    )
```

```python
import functools
import itertools

import jax
import jax.numpy as jnp
from jax import lax
from jax.experimental import pallas as pl
from jax.experimental.pallas import tpu as pltpu
from jax.sharding import PartitionSpec as P

DH = 128
EPSILON = 1e-06
SIDE = 4
SPLIT = (1, 2, 2)
PAIR = 2
HOPS = (0, 1, 2, 1)
MESH = pl.DeviceIdType.MESH
F32 = jnp.float32
BF16 = jnp.bfloat16
NN = ((1,), (0,))
NT = ((1,), (1,))
TN = ((0,), (0,))


def dot(a, b, dims):
    return lax.dot_general(a, b, (dims, ((), ())), preferred_element_type=F32)


def routes(place, group, split):
    per_axis = []
    for at, chosen, part in zip(place, group, split):
        steps = []
        for turn in range(SIDE // part):
            shift = (chosen - at) % part + part * turn
            hops = sum(HOPS[part * turn + i] for i in range(part)) / part
            steps.append(((at + shift) % SIDE, hops, turn == 0))
        per_axis.append(steps)
    found = []
    for steps in itertools.product(*per_axis):
        ctx, member = 0, 0
        for (at, _, _), part in zip(steps, split):
            ctx = ctx * SIDE + at
            member = member * (SIDE // part) + at // part
        found.append((sum(s[1] for s in steps), ctx, member, all(s[2] for s in steps)))
    found.sort(key=lambda r: -r[0])
    return [r[1:] for r in found]


def parts_of(a):
    hi = a.astype(BF16)
    rest = a - hi.astype(F32)
    mid = rest.astype(BF16)
    return [hi, mid, (rest - mid.astype(F32)).astype(BF16)]


def along_lanes(a):
    ones = jnp.ones((8, a.shape[1]), BF16)
    return sum(dot(ones, part, NT) for part in parts_of(a))


def kernel(
    n, heads, pos,
    q_hbm, k_hbm, v_hbm, ld_hbm, gain_hbm, g_hbm,
    out, gq, gk, gv,
    q, k, v, g, ld, gain,
    cum, trail_h, kt, cumb, leadb, trailb, decay, weights, dk, dv, ql, qt,
    attn, gg, d_attn,
    s_send, s_recv, e_send, e_recv, t_send, t_recv, l_send, l_recv,
    totals, block_decay, sums, sums_in, scaleb, pullb,
    in_sem, share_sem, group_sem, sum_sem,
):
    c = lax.axis_index("ctx")
    core = lax.axis_index("head")
    place = (c // (SIDE * SIDE), (c // SIDE) % SIDE, c % SIDE)
    rows = DH * heads // n
    per_head = n // heads
    groups = list(itertools.product(*(range(part) for part in SPLIT)))
    members = n // len(groups)
    group_heads = heads // len(groups)
    my_group, my_member = 0, 0
    for at, part in zip(place, SPLIT):
        my_group = my_group * part + at % part
        my_member = my_member * (SIDE // part) + at // part
    mine = my_group * members + my_member
    width = heads * DH

    loads = [
        pltpu.make_async_copy(src, dst, in_sem.at[i])
        for i, (src, dst) in enumerate(
            ((ld_hbm, ld), (k_hbm, k), (v_hbm, v), (q_hbm, q), (gain_hbm, gain), (g_hbm, g))
        )
    ]
    for load in loads:
        load.start()

    barrier = pltpu.get_barrier_semaphore()

    def greet(i, _):
        pl.semaphore_signal(
            barrier, inc=1, device_id=((c + i) % n, core), device_id_type=MESH
        )
        return 0

    lax.fori_loop(1, n, greet, 0)
    pl.semaphore_signal(barrier, inc=1, device_id=(c, 1 - core), device_id_type=MESH)

    def lanes(h):
        return pl.ds(h * DH, DH) if isinstance(h, int) else pl.ds(pl.multiple_of(h * DH, DH), DH)

    def shares(h):
        return pl.ds(h * per_head, per_head)

    def send(src, dst, sent, landed, dest, maybe_me):
        def away():
            pltpu.make_async_remote_copy(
                src_ref=src, dst_ref=dst, send_sem=sent, recv_sem=landed,
                device_id=(dest, core), device_id_type=MESH,
            ).start()

        if maybe_me:
            pl.when(dest != c)(away)

            @pl.when(dest == c)
            def _():
                pltpu.make_async_copy(src, dst, landed).start()
        else:
            away()

    def to_owners(src, dst, which, group):
        for dest, member, maybe_me in routes(place, groups[group], SPLIT):
            send(
                src.at[group * members + member], dst.at[c],
                share_sem.at[2 * which], share_sem.at[2 * which + 1], dest, maybe_me,
            )

    def from_owner(src, dst, which):
        for dest, _, maybe_me in routes(place, (0, 0, 0), (1, 1, 1)):
            send(
                src.at[dest], dst.at[mine],
                share_sem.at[4 + which], group_sem.at[which, my_group], dest, maybe_me,
            )

    def any_copy(ref, sent, landed):
        return pltpu.make_async_remote_copy(
            src_ref=ref, dst_ref=ref, send_sem=sent, recv_sem=landed,
            device_id=((c + 1) % n, core), device_id_type=MESH,
        )

    def owners_wait(dst, which):
        any_copy(dst, share_sem.at[2 * which], share_sem.at[2 * which + 1]).wait_recv()

    def group_wait(dst, which, group):
        any_copy(
            dst.at[pl.ds(group * members, members)],
            share_sem.at[4 + which], group_sem.at[which, group],
        ).wait_recv()

    def each(first, last, body, unroll):
        def step(h, _):
            body(h)
            return 0

        lax.fori_loop(first, last, step, 0, unroll=unroll)

    t_i = lax.broadcasted_iota(jnp.int32, (pos, pos), 0)
    s_i = lax.broadcasted_iota(jnp.int32, (pos, pos), 1)
    lower = jnp.where(t_i >= s_i, 1.0, 0.0).astype(BF16)

    loads[0].wait()
    ld_all = ld[...]
    hi = ld_all.astype(BF16)
    rest = ld_all - hi.astype(F32)
    mid = rest.astype(BF16)
    low = (rest - mid.astype(F32)).astype(BF16)
    parts = jnp.concatenate([hi, mid, low], axis=0)
    summed = dot(parts, lower, NT)
    cum_h = summed[:heads] + summed[heads : 2 * heads] + summed[2 * heads :]
    cum[...] = cum_h
    trail_h[...] = jnp.exp(cum_h[:, pos - 1 :] - cum_h)
    my_row = totals.at[c // 8, c % 8]
    padded = jnp.concatenate([cum_h[:, pos - DH :], jnp.zeros((DH - heads, DH), F32)], axis=0)
    my_row[...] = padded.T[DH - 1 :, :]

    loads[1].wait()

    def turn(h):
        kt[h] = k[:, lanes(h)].T

    each(0, heads, turn, 4)
    loads[2].wait()

    def own_state(h):
        keys = (kt[h].astype(F32) * trail_h[pl.ds(h, 1), :]).astype(BF16)
        state = dot(keys, v[:, lanes(h)], NN).astype(BF16)
        s_send[shares(h)] = state.reshape(per_head, rows, DH)

    def send_totals():
        for i in range(1, 8):
            pltpu.make_async_remote_copy(
                src_ref=my_row, dst_ref=my_row,
                send_sem=sum_sem.at[2], recv_sem=sum_sem.at[3],
                device_id=((c // 8) * 8 + (c + i) % 8, core), device_id_type=MESH,
            ).start()

    each(0, heads, own_state, 4)
    pl.semaphore_wait(barrier, n)
    send_totals()
    for group in range(len(groups)):
        to_owners(s_send, s_recv, 0, group)

    parts = jnp.concatenate([parts, jnp.zeros((DH - 3 * heads, pos), BF16)], axis=0)
    summed = dot(lower, parts, NT)
    cum_t = summed[:, :heads] + summed[:, heads : 2 * heads] + summed[:, 2 * heads : 3 * heads]
    trail_t = jnp.exp(cum_t[pos - 1 :, :] - cum_t)
    lead_t = jnp.exp(cum_t)
    for h in range(heads):
        cumb[h] = jnp.broadcast_to(cum_t[:, h : h + 1], (pos, DH))
        leadb[h] = jnp.broadcast_to(lead_t[:, h : h + 1], (pos, DH))
        trailb[h] = jnp.broadcast_to(trail_t[:, h : h + 1], (pos, DH))

    loads[3].wait()

    def inside(h):
        scores = dot(q[:, lanes(h)], k[:, lanes(h)], NT)
        row = cum[pl.ds(h, 1), :]
        col = cumb[h]
        spread = jnp.concatenate([col, col], axis=1) - row
        d = jnp.exp(jnp.where(t_i >= s_i, spread, -1e30))
        decay[h] = d
        w = (scores * d).astype(BF16)
        weights[h] = w
        attn[:, lanes(h)] = dot(w, v[:, lanes(h)], NN)
        lead_q = (q[:, lanes(h)].astype(F32) * leadb[h]).astype(BF16)
        ql[:, lanes(h)] = lead_q
        qt[h] = lead_q.T

    each(0, heads // 8, inside, 2)

    any_copy(totals.at[0, pl.ds(0, 7)], sum_sem.at[2], sum_sem.at[3]).wait()
    for i in range(1, 8):
        pltpu.make_async_remote_copy(
            src_ref=totals.at[c // 8], dst_ref=totals.at[c // 8],
            send_sem=sum_sem.at[4], recv_sem=sum_sem.at[5],
            device_id=((c // 8 + i) % 8 * 8 + c % 8, core), device_id_type=MESH,
        ).start()

    each(heads // 8, heads // 2, inside, 2)

    any_copy(totals.at[pl.ds(0, 7)], sum_sem.at[4], sum_sem.at[5]).wait()
    every = totals[...].reshape(n, DH)
    lane_i = lax.broadcasted_iota(jnp.int32, (n, DH), 1)
    total = jnp.sum(jnp.where(lane_i == mine // per_head, every, 0.0), axis=1, keepdims=True)
    block_decay[...] = jnp.broadcast_to(jnp.exp(total), (n, DH))

    def scan(src, dst, reverse):
        def one(i, state):
            j = n - 1 - i if reverse else i
            dst[j] = state.astype(BF16)
            return state * block_decay[pl.ds(j, 1), :] + src[j].astype(F32)

        lax.fori_loop(0, n, one, jnp.zeros((rows, DH), F32), unroll=16)

    owners_wait(s_recv, 0)
    scan(s_recv, e_send, False)
    from_owner(e_send, e_recv, 0)

    each(heads // 2, heads, inside, 2)
    loads[4].wait()
    loads[5].wait()

    def prepare(h):
        gg[:, lanes(h)] = gain[:, lanes(h)] * g[:, lanes(h)].astype(F32)
        dk[:, lanes(h)] = (k[:, lanes(h)].astype(F32) * trailb[h]).astype(BF16)
        dv[:, lanes(h)] = (v[:, lanes(h)].astype(F32) * trailb[h]).astype(BF16)

    each(0, heads, prepare, 2)

    def attend(h, carry):
        squares, inner = carry
        entering = e_recv[shares(h)].reshape(DH, DH)
        a = attn[:, lanes(h)] + dot(ql[:, lanes(h)], entering, NN)
        attn[:, lanes(h)] = a
        return squares + a * a, inner + a * gg[:, lanes(h)]

    squares = inner = jnp.zeros((pos, DH), F32)
    for group in range(0, len(groups), PAIR):
        for i in range(PAIR):
            group_wait(e_recv, 0, group + i)
        squares, inner = lax.fori_loop(
            group * group_heads, (group + PAIR) * group_heads, attend, (squares, inner),
            unroll=PAIR * group_heads,
        )
    sums[...] = jnp.concatenate([along_lanes(squares), along_lanes(inner)], axis=0)
    swap = pltpu.make_async_remote_copy(
        src_ref=sums, dst_ref=sums_in, send_sem=sum_sem.at[0], recv_sem=sum_sem.at[1],
        device_id=(c, 1 - core), device_id_type=MESH,
    )
    swap.start()
    swap.wait()
    both = (sums[...] + sums_in[...]) / (2 * width)
    scale = lax.rsqrt(both[:8] + EPSILON)
    pull = scale * scale * scale * both[8:]
    part_i = lax.broadcasted_iota(jnp.int32, (48, 2 * DH), 0)
    lane_i = lax.broadcasted_iota(jnp.int32, (48, 2 * DH), 1)
    chosen = (part_i % 8 == 0) & ((part_i < 24) == (lane_i < DH))
    both = dot(
        jnp.concatenate(parts_of(scale) + parts_of(pull), axis=0),
        jnp.where(chosen, 1.0, 0.0).astype(BF16), TN,
    )
    scaleb[...] = both[:, :DH]
    pullb[...] = both[:, DH:]

    def own_grad(h):
        d = (scaleb[...] * gg[:, lanes(h)] - attn[:, lanes(h)] * pullb[...]).astype(BF16)
        d_attn[:, lanes(h)] = d
        state = dot(qt[h], d, NN).astype(BF16)
        t_send[shares(h)] = state.reshape(per_head, rows, DH)

    for group in range(0, len(groups), PAIR):
        each(group * group_heads, (group + PAIR) * group_heads, own_grad, PAIR * group_heads)
        for i in range(PAIR):
            to_owners(t_send, t_recv, 1, group + i)

    def gradients(h):
        d = d_attn[:, lanes(h)]
        out[:, lanes(h)] = (attn[:, lanes(h)] * scaleb[...] * gain[:, lanes(h)]).astype(BF16)
        w = weights[h]
        gw = (dot(d, v[:, lanes(h)], NT) * decay[h]).astype(BF16)
        entering = e_recv[shares(h)].reshape(DH, DH)
        gq[:, lanes(h)] = (
            leadb[h] * dot(d, entering, NT) + dot(gw, k[:, lanes(h)], NN)
        ).astype(BF16)
        attn[:, lanes(h)] = dot(gw, q[:, lanes(h)], TN)
        decay[h, :, 0:DH] = dot(w, d, TN)

    each(0, heads // 2, gradients, 1)
    owners_wait(t_recv, 1)
    scan(t_recv, l_send, True)
    from_owner(l_send, l_recv, 1)
    each(heads // 2, heads, gradients, 1)

    def finish(h):
        leaving = l_recv[shares(h)].reshape(DH, DH)
        gk[:, lanes(h)] = (attn[:, lanes(h)] + dot(dv[:, lanes(h)], leaving, NT)).astype(BF16)
        gv[:, lanes(h)] = (decay[h, :, 0:DH] + dot(dk[:, lanes(h)], leaving, NN)).astype(BF16)

    for group in range(0, len(groups), PAIR):
        for i in range(PAIR):
            group_wait(l_recv, 1, group + i)
        each(group * group_heads, (group + PAIR) * group_heads, finish, PAIR * group_heads)

    for which, ref in enumerate((s_send, t_send, e_send, l_send)):
        any_copy(ref.at[pl.ds(0, n - 1)], share_sem.at[(0, 2, 4, 5)[which]], share_sem.at[1]).wait_send()


def write_out(*refs):
    copies = [
        pltpu.make_async_copy(src, dst, refs[8].at[i])
        for i, (src, dst) in enumerate(zip(refs[:4], refs[4:8]))
    ]
    for copy in copies:
        copy.start()
    for copy in copies:
        copy.wait()


def solution(mesh):
    n = mesh.shape["ctx"]

    def local(queries, keys, values, log_decay, norm_gain, d_out):
        pos, width = queries.shape
        heads = width // DH
        rows = DH * heads // n
        wide = jax.ShapeDtypeStruct((pos, width), BF16)
        hbm = pl.BlockSpec(memory_space=pltpu.HBM)
        vmem = pl.BlockSpec(memory_space=pltpu.VMEM)
        shares = pltpu.VMEM((n, rows, DH), BF16)
        columns = pltpu.VMEM((heads, pos, DH), F32)
        flat = pltpu.VMEM((pos, width), BF16)
        flat_f32 = pltpu.VMEM((pos, width), F32)
        small = pltpu.VMEM((pos, DH), F32)
        held = pl.pallas_call(
            functools.partial(kernel, n, heads, pos),
            out_shape=[pltpu.VMEM((pos, width), BF16)] * 4,
            in_specs=[hbm] * 6,
            out_specs=[vmem] * 4,
            scratch_shapes=[
                flat, flat, flat, flat,
                pltpu.VMEM((heads, pos), F32),
                pltpu.VMEM((1, width), F32),
                pltpu.VMEM((heads, pos), F32),
                pltpu.VMEM((heads, pos), F32),
                pltpu.VMEM((heads, DH, pos), BF16),
                columns, columns, columns,
                pltpu.VMEM((heads, pos, pos), F32),
                pltpu.VMEM((heads, pos, pos), BF16),
                flat, flat, flat,
                pltpu.VMEM((heads, DH, pos), BF16),
                flat_f32, flat_f32, flat,
                shares, shares, shares, shares, shares, shares, shares, shares,
                pltpu.VMEM((8, n // 8, 1, DH), F32),
                pltpu.VMEM((n, DH), F32),
                pltpu.VMEM((16, pos), F32),
                pltpu.VMEM((16, pos), F32),
                small, small,
                pltpu.SemaphoreType.DMA((6,)),
                pltpu.SemaphoreType.DMA((6,)),
                pltpu.SemaphoreType.DMA((2, SPLIT[0] * SPLIT[1] * SPLIT[2])),
                pltpu.SemaphoreType.DMA((6,)),
            ],
            compiler_params=pltpu.CompilerParams(
                collective_id=0, has_side_effects=True, vmem_limit_bytes=44 * 2**20
            ),
            cost_estimate=pl.CostEstimate(
                flops=36 * pos * DH * DH * heads, bytes_accessed=16 * pos * width, transcendentals=0
            ),
            name="attention",
        )(*(pltpu.with_memory_space_constraint(a, pltpu.HBM) for a in (queries, keys, values, log_decay, norm_gain.reshape(1, width), d_out)))
        return pl.pallas_call(
            write_out,
            out_shape=[wide] * 4,
            in_specs=[pl.BlockSpec(memory_space=pl.ANY)] * 4,
            out_specs=[hbm] * 4,
            scratch_shapes=[pltpu.SemaphoreType.DMA((4,))],
            compiler_params=pltpu.CompilerParams(vmem_limit_bytes=16 * 2**20),
            name="write_out",
        )(*(pltpu.with_memory_space_constraint(a, pltpu.VMEM) for a in held))

    wide = P("ctx", "head")
    return jax.shard_map(
        local,
        mesh=mesh,
        in_specs=(wide, wide, wide, P("head", "ctx"), P("head"), wide),
        out_specs=(wide, wide, wide, wide),
        check_vma=False,
    )
```
